32 devices in a mesh: rows: 8 (over y, x, core), rep: 4 (over z).
Axes of the slice: x: 2, y: 2, z: 4, core: 2. Of those that a mesh axis runs over, the one named last changes fastest.
Arguments:
- weights: bfloat16 [80, 524288], P('rep', 'rows'), may hold values from 0.25 to 4
- cell_ids: int32 [524288], P('rows'), may hold values from 0 to 31
- group_sizes: int32 [8, 1024], P('rows'), may hold values from 32 to 96, as said below
- group_county: int32 [8192, 1], P('rows'), may hold values from 0 to 255; in each aligned block of 1024 rows (0 to 1023, 1024 to 2047, ...) at most 10 rows name the same one
- age_rate: float32 [256, 4], P('rows'), may hold values from 8 to 40
- kind_rate: float32 [256, 8], P('rows'), may hold values from 2 to 20
Outputs:
- raked: float32 [8192, 2560], P('rows', 'rep')
- spread: float32 [8192, 32], P('rows')
The draws below stay inside these ranges and needn't reach their ends.
Inputs may be any that keep to these rules, and one draw needn't show every extreme that they name: `group_sizes`: each shard's 1024 sizes sum to 65536. `group_county`: among the 1024 block groups of one shard, no county holds more than 10.
All inputs are finite; a program needn't handle non-finite values.
Results may differ from the reference program's by a relative error of at most 0.0003.
Values sent between devices are 32-bit elements; how exact they have to be, the bound alone decides.
A program may use at most 64 MiB of HBM per device.

```python
import math
import jax
import jax.numpy as jnp
import numpy as np
from jax import lax

REPS = 80
AGES = 4
KINDS = 8
CELLS = 32
LOW = 32
HIGH = 96
ITERS = 4
BG_DEV = 1024
SHARDS = 8
BGROUPS = 8192
RECORDS = 524288
COUNTIES = 256
PAIR = 10


def draw_cell_ids(key, part):
    key_perm, key_base, key_pick = jax.random.split(key, 3)
    kind_order = jax.random.permutation(key_perm, KINDS).astype(jnp.int32)
    tied_age = kind_order % AGES
    age_range = jnp.arange(AGES, dtype=jnp.int32)
    tied = (tied_age[None, :] == age_range[:, None]).astype(jnp.int32)
    base = jax.random.randint(key_base, (AGES, KINDS), 1, 4).astype(jnp.int32)
    cell_weight = (base + 24 * tied).reshape(-1)
    cumulative = jnp.cumsum(cell_weight).astype(jnp.int32)
    total = cumulative[-1]
    picks = jax.random.randint(key_pick, (RECORDS,), 0, total).astype(jnp.int32)
    return jnp.searchsorted(cumulative, picks, side='right').astype(jnp.int32)


def draw_group_sizes(key, part):
    key_a, key_b = jax.random.split(key)
    half_span = (HIGH - LOW) // 2
    middle = (HIGH + LOW) // 2
    raised = jax.random.randint(key_a, (SHARDS, BG_DEV), 0, half_span + 1)
    offset = jax.random.randint(key_b, (SHARDS, 1), 1, BG_DEV)
    column = jnp.arange(BG_DEV, dtype=jnp.int32)[None, :]
    raised = jnp.where(column == 0, half_span, raised)
    raised = jnp.where(column == offset, 0, raised)
    raised = jnp.where(column == BG_DEV - offset, 0, raised)
    partner = jnp.take_along_axis(raised, (column + offset) % BG_DEV, axis=1)
    return (middle + raised - partner).astype(jnp.int32)


def block_scale(own_key, shape, shards, least, largest):
    gain, own = 1.0, jax.random.fold_in(own_key, 6)
    for dim, shards_of in shards:
        heights = jnp.exp(jax.random.uniform(jax.random.fold_in(own, dim), (shards_of,), jnp.float32, least / len(shards), largest / len(shards)))
        gain = gain * jnp.repeat(heights, shape[dim] // shards_of).reshape([-1 if axis == dim else 1 for axis in range(len(shape))])
    return gain


def assign_block(key, own, number, rows, amount, top, reach, slope):
    sequence = jax.random.permutation(key, amount)
    heavy_load, ordinary = portions_of(amount, rows * top, reach, slope, True), portions_of(amount, rows * top, reach, slope, False)
    places = jnp.arange(amount)

    def named(tallies, rotation):
        used = int((tallies > 0).sum())
        fixed = max(1, used // 4)
        shifted = fixed + (places - fixed + rotation * (used - fixed)) % max(1, amount - fixed)
        return jnp.zeros((amount,), jnp.int32).at[sequence[jnp.where(places < fixed, places, shifted)]].set(jnp.asarray(tallies, jnp.int32))

    tallies = jnp.where(number % 4 == 0, named(heavy_load, number // 4), named(ordinary, number - number // 4 - 1))
    mixed = jax.random.permutation(jax.random.fold_in(own, 3), amount)
    giver, receiver = mixed[0:amount // 2 * 2:2], mixed[1:amount // 2 * 2:2]
    room = jnp.minimum(tallies[giver] - 1, reach - tallies[receiver]) // 2
    room = jnp.where((giver == sequence[0]) | (receiver == sequence[0]) | (tallies[receiver] == 0), 0, jnp.maximum(room, 0))
    shifted = jax.random.randint(jax.random.fold_in(own, 4), (amount // 2,), 0, 1 << 20) % (room + 1)
    tallies = tallies.at[giver].add(-shifted).at[receiver].add(shifted)
    labels = jnp.searchsorted(jnp.cumsum(tallies), jnp.arange(rows * top), side="right").astype(jnp.int32)
    listing = labels.reshape(top, rows).T
    listing = listing[jax.random.permutation(jax.random.fold_in(own, 1), rows)]
    rotation = jax.random.randint(jax.random.fold_in(own, 2), (rows, 1), 0, top)
    return jnp.take_along_axis(listing, (jnp.arange(top)[None, :] + rotation) % top, axis=1)


def portions_of(amount, total, bound, slope, full):
    weights = [(1 << 20) // math.isqrt(rank ** slope) + 1 for rank in range(1, amount + 1)]
    largest = bound if full else min(bound, max(-(-total // amount), total * weights[0] // sum(weights)))
    least = 1 if total - largest >= amount - 1 else 0
    holding, rest = [largest] + [least] * (amount - 1), total - largest - least * (amount - 1)
    while rest > 0:
        free = [i for i in range(1, amount) if holding[i] < largest] or [i for i in range(1, amount) if holding[i] < bound]
        mass, remaining = sum([weights[i] for i in free]), rest
        for i in free:
            extra = min(bound - holding[i], max(1, remaining * weights[i] // mass), rest)
            holding[i] = holding[i] + extra
            rest = rest - extra
    return np.array(holding)


def setup_inputs(seed: int = 0) -> dict:
    keys = jax.random.split(jax.random.key(seed), 7)
    weights = jnp.clip(jnp.exp(math.log(4.0) - 2.7725887 * jax.random.uniform(keys[0], (REPS, RECORDS), jnp.float32) ** block_scale(keys[0], (REPS, RECORDS), ((0, 4), (1, 8)), -0.2, 0.2)), 0.25, 4.0).astype(jnp.bfloat16)
    cell_ids = draw_cell_ids(jax.random.fold_in(keys[6], 71), 0)
    group_sizes = draw_group_sizes(jax.random.fold_in(keys[6], 71), 0)
    group_county_keys = jax.random.split(jax.random.fold_in(keys[3], 1), BGROUPS // BG_DEV)
    group_county_turns = jax.random.permutation(jax.random.fold_in(keys[3], 3), BGROUPS // BG_DEV)
    group_county = jax.vmap(lambda own, number: assign_block(jax.random.fold_in(keys[3], 2), own, number, BG_DEV, COUNTIES, 1, PAIR, 1))(group_county_keys, group_county_turns).reshape((BGROUPS, 1))
    age_rate = jnp.clip(jnp.exp(math.log(40.0) - 1.609438 * jax.random.uniform(keys[4], (COUNTIES, AGES), jnp.float32) ** block_scale(keys[4], (COUNTIES, AGES), ((0, 8),), -0.2, 0.2)), 8.0, 40.0)
    kind_rate = jnp.clip(jnp.exp(math.log(20.0) - 2.3025851 * jax.random.uniform(keys[5], (COUNTIES, KINDS), jnp.float32) ** block_scale(keys[5], (COUNTIES, KINDS), ((0, 8),), -0.2, 0.2)), 2.0, 20.0)
    return dict(weights=weights, cell_ids=cell_ids, group_sizes=group_sizes, group_county=group_county, age_rate=age_rate, kind_rate=kind_rate)


def rake(county_tables, groups_in, age_rate, kind_rate):
    county_rows = county_tables.shape[0]
    current = county_tables.reshape(county_rows, -1, AGES, KINDS)
    age_goal = (age_rate * groups_in[:, None])[:, None, :]
    kind_goal = (kind_rate * groups_in[:, None])[:, None, :]
    factor = jnp.ones_like(current)
    for sweep_index in range(ITERS):
        ratios = age_goal / jnp.maximum(jnp.sum(current, axis=3), 1.0)
        current = current * ratios[:, :, :, None]
        factor = factor * ratios[:, :, :, None]
        ratios = kind_goal / jnp.maximum(jnp.sum(current, axis=2), 1.0)
        current = current * ratios[:, :, None, :]
        factor = factor * ratios[:, :, None, :]
    return factor.reshape(county_rows, -1)


def reference(weights, cell_ids, group_sizes, group_county, age_rate, kind_rate):
    sizes_flat = group_sizes.reshape(-1)
    group_of = jnp.repeat(jnp.arange(BGROUPS, dtype=jnp.int32), sizes_flat, total_repeat_length=RECORDS).astype(jnp.int32)
    segment_ids = group_of * CELLS + cell_ids

    def per_replicate(weight_row):
        return jax.ops.segment_sum(weight_row.astype(jnp.float32), segment_ids, num_segments=BGROUPS * CELLS)

    per_rep = lax.map(per_replicate, weights)
    tables = per_rep.reshape(REPS, BGROUPS, CELLS).transpose(1, 0, 2).reshape(BGROUPS, REPS * CELLS)
    county_ids = group_county[:, 0]
    county_tables = jax.ops.segment_sum(tables, county_ids, num_segments=COUNTIES)
    groups_in = jax.ops.segment_sum(jnp.ones((BGROUPS,), jnp.float32), county_ids, num_segments=COUNTIES)
    factor = rake(county_tables, groups_in, age_rate, kind_rate)
    raked = tables * factor[county_ids]
    shaped = raked.reshape(BGROUPS, REPS, CELLS)
    centre = jnp.sum(shaped, axis=1) / REPS
    spread = jnp.sum(jnp.square(shaped - centre[:, None, :]), axis=1) * (4.0 / REPS)
    return raked, spread
```

```python
import jax
import jax.numpy as jnp
from jax import lax
from jax.experimental import pallas as pl
from jax.experimental.pallas import tpu as pltpu
from jax.sharding import PartitionSpec as P

AGES = 4
KINDS = 8
CELLS = 32
LOW = 32
ITERS = 4
BLOCK = 1024
HALF = CELLS // 2
TILE = 128


def rake(county_tables, groups_in, age_rate, kind_rate):
    county_rows = county_tables.shape[0]
    current = county_tables.reshape(county_rows, -1, AGES, KINDS)
    age_goal = (age_rate * groups_in[:, None])[:, None, :]
    kind_goal = (kind_rate * groups_in[:, None])[:, None, :]
    factor = jnp.ones_like(current)
    for sweep_index in range(ITERS):
        ratios = age_goal / jnp.maximum(jnp.sum(current, axis=3), 1.0)
        current = current * ratios[:, :, :, None]
        factor = factor * ratios[:, :, :, None]
        ratios = kind_goal / jnp.maximum(jnp.sum(current, axis=2), 1.0)
        current = current * ratios[:, :, None, :]
        factor = factor * ratios[:, :, None, :]
    return factor.reshape(county_rows, -1)


def exact_dot(left, right):
    return jnp.dot(left, right, precision=lax.Precision.HIGHEST, preferred_element_type=jnp.float32)


def tabulate_kernel(starts, first, low, high, weights, cells, out, group_of, total):
    tile = pl.program_id(0)
    reps = weights.shape[0]
    blocks = weights.shape[1] // BLOCK
    rows = BLOCK // 128

    @pl.when(tile == 0)
    def _():
        place0 = lax.broadcasted_iota(jnp.int32, (rows, 128), 0) * 128 + lax.broadcasted_iota(
            jnp.int32, (rows, 128), 1
        )

        def name(i, carry):
            place = place0 + i * BLOCK
            g0 = first[i]
            count = jnp.full((rows, 128), g0, jnp.int32)
            for j in range(BLOCK // LOW):
                count = count + (place >= starts[g0 + 1 + j]).astype(jnp.int32)
            group_of[pl.ds(i * rows, rows), :] = count
            return carry

        lax.fori_loop(0, blocks, name, 0)

    total[...] = jnp.zeros_like(total)
    slot = lax.broadcasted_iota(jnp.int32, (2 * TILE, 128), 0).astype(jnp.float32).astype(jnp.bfloat16)
    low_slot = lax.broadcasted_iota(jnp.int32, (HALF, 128), 0).astype(jnp.float32).astype(jnp.bfloat16)
    one = jnp.ones((2 * TILE, 128), jnp.bfloat16)
    zero = jnp.zeros((2 * TILE, 128), jnp.bfloat16)
    nothing = jnp.zeros((HALF, 128), jnp.bfloat16)

    def add_block(i, carry):
        base = pl.multiple_of(i * rows, rows)
        cell = cells[pl.ds(base, rows), :]
        near = group_of[pl.ds(base, rows), :] - tile * TILE
        inside = (near >= 0) & (near < TILE)
        place = jnp.where(inside, near + (cell // HALF) * TILE, -1).astype(jnp.float32)
        inner = (cell % HALF).astype(jnp.float32)
        lefts, rights = [], []
        for j in range(rows):
            lanes = pl.ds(pl.multiple_of(i * BLOCK + j * 128, 128), 128)
            w = weights[:, lanes].astype(jnp.float32)
            here = jnp.broadcast_to(place[j : j + 1, :], (2 * TILE, 128)).astype(jnp.bfloat16)
            rights.append(jnp.where(here == slot, one, zero))
            mask = jnp.broadcast_to(inner[j : j + 1, :], (HALF, 128)).astype(jnp.bfloat16) == low_slot
            lefts.append(
                jnp.concatenate(
                    [
                        jnp.where(
                            mask,
                            jnp.broadcast_to(w[r : r + 1, :], (HALF, 128)).astype(jnp.bfloat16),
                            nothing,
                        )
                        for r in range(reps)
                    ],
                    axis=0,
                )
            )
        left = jnp.concatenate(lefts, axis=1)
        right = jnp.concatenate(rights, axis=1)
        total[...] += lax.dot_general(
            left, right, (((1,), (1,)), ((), ())), preferred_element_type=jnp.float32
        )
        return carry

    lax.fori_loop(low[tile], high[tile], add_block, 0)
    for r in range(reps):
        for h in range(2):
            out[r * CELLS + h * HALF : r * CELLS + (h + 1) * HALF, :] = total[
                r * HALF : (r + 1) * HALF, h * TILE : (h + 1) * TILE
            ]


def tabulate(weights, cell_ids, group_sizes):
    reps, records = weights.shape
    groups = group_sizes.shape[1]
    blocks = records // BLOCK
    group_range = jnp.arange(groups, dtype=jnp.int32)
    upper = (group_range[:, None] <= group_range[None, :]).astype(jnp.float32)
    ends = exact_dot(group_sizes.astype(jnp.float32), upper)[0].astype(jnp.int32)
    starts = ends - group_sizes[0]
    edge = jnp.arange(blocks, dtype=jnp.int32) * BLOCK
    first = jnp.sum((ends[None, :] <= edge[:, None]).astype(jnp.int32), axis=1)
    low = starts[::TILE] // BLOCK
    high = (ends[TILE - 1 :: TILE] + BLOCK - 1) // BLOCK
    starts = jnp.concatenate([starts, jnp.full((128,), records + 1, jnp.int32)])
    smem = pl.BlockSpec(memory_space=pltpu.SMEM)
    return pl.pallas_call(
        tabulate_kernel,
        out_shape=jax.ShapeDtypeStruct((reps * CELLS, groups), jnp.float32),
        grid=(groups // TILE,),
        in_specs=[
            smem,
            smem,
            smem,
            smem,
            pl.BlockSpec((reps, records), lambda t: (0, 0)),
            pl.BlockSpec((records // 128, 128), lambda t: (0, 0)),
        ],
        out_specs=pl.BlockSpec((reps * CELLS, TILE), lambda t: (0, t)),
        scratch_shapes=[
            pltpu.VMEM((records // 128, 128), jnp.int32),
            pltpu.VMEM((reps * HALF, 2 * TILE), jnp.float32),
        ],
        compiler_params=pltpu.CompilerParams(vmem_limit_bytes=40 * 1024 * 1024),
    )(starts, first, low, high, weights, cell_ids.reshape(records // 128, 128))


def local(weights, cell_ids, group_sizes, group_county, age_rate, kind_rate):
    tables = tabulate(weights, cell_ids, group_sizes).T
    group_here, row_width = tables.shape
    county_ids = group_county[:, 0]
    owners = lax.axis_size("rows")
    county_here = age_rate.shape[0]
    counties = county_here * owners
    county_range = jnp.arange(counties, dtype=jnp.int32)
    county_hot = (county_ids[:, None] == county_range[None, :]).astype(jnp.float32)
    partial_value = exact_dot(county_hot.T, tables)
    member = jnp.sum(county_hot, axis=0)
    county_tables = lax.psum_scatter(partial_value, "rows", scatter_dimension=0, tiled=True)
    groups_in = lax.psum_scatter(member, "rows", scatter_dimension=0, tiled=True)
    factor = rake(county_tables, groups_in, age_rate, kind_rate)
    all_factors = lax.all_gather(factor, "rows", axis=0, tiled=True)
    raked = tables * exact_dot(county_hot, all_factors)
    reps_here = row_width // CELLS
    shaped = raked.reshape(group_here, reps_here, CELLS)
    parts = lax.axis_size("rep")
    total_reps = reps_here * parts
    mean = jnp.sum(shaped, axis=1) / reps_here
    within = jnp.sum(jnp.square(shaped - mean[:, None, :]), axis=1)
    both = lax.all_gather(jnp.stack([mean.T, within.T]), "rep", axis=0)
    means, withins = both[:, 0], both[:, 1]
    centre = jnp.sum(means, axis=0) / parts
    deviation = jnp.sum(withins + reps_here * jnp.square(means - centre[None]), axis=0)
    return (raked, deviation.T * (4.0 / total_reps))


def solution(mesh):
    placed = (
        P("rep", "rows"),
        P("rows"),
        P("rows", None),
        P("rows", None),
        P("rows", None),
        P("rows", None),
    )
    return jax.shard_map(
        local,
        mesh=mesh,
        in_specs=placed,
        out_specs=(P("rows", "rep"), P("rows", None)),
        check_vma=False,
    )
```

```python
import functools

import jax
import jax.numpy as jnp
from jax import lax
from jax.experimental import pallas as pl
from jax.experimental.pallas import tpu as pltpu
from jax.sharding import PartitionSpec as P

AGES = 4
KINDS = 8
CELLS = 32
LOW = 32
ITERS = 4
BLOCK = 1024
HALF = CELLS // 2
TILE = 128
MESH = pl.DeviceIdType.MESH


def exact_dot(left, right):
    return jnp.dot(left, right, precision=lax.Precision.HIGHEST, preferred_element_type=jnp.float32)


def tabulate_kernel(starts, first, low, high, weights, cells, out, group_of, total):
    tile = pl.program_id(0)
    reps = weights.shape[0]
    blocks = weights.shape[1] // BLOCK
    rows = BLOCK // 128

    @pl.when(tile == 0)
    def _():
        place0 = lax.broadcasted_iota(jnp.int32, (rows, 128), 0) * 128 + lax.broadcasted_iota(
            jnp.int32, (rows, 128), 1
        )

        def name(i, carry):
            place = place0 + i * BLOCK
            g0 = first[i]
            count = jnp.full((rows, 128), g0, jnp.int32)
            for j in range(BLOCK // LOW):
                count = count + (place >= starts[g0 + 1 + j]).astype(jnp.int32)
            group_of[pl.ds(i * rows, rows), :] = count
            return carry

        lax.fori_loop(0, blocks, name, 0)

    total[...] = jnp.zeros_like(total)
    slot = lax.broadcasted_iota(jnp.int32, (2 * TILE, 128), 0).astype(jnp.float32).astype(jnp.bfloat16)
    low_slot = lax.broadcasted_iota(jnp.int32, (HALF, 128), 0).astype(jnp.float32).astype(jnp.bfloat16)
    one = jnp.ones((2 * TILE, 128), jnp.bfloat16)
    zero = jnp.zeros((2 * TILE, 128), jnp.bfloat16)
    nothing = jnp.zeros((HALF, 128), jnp.bfloat16)

    def add_block(i, carry):
        base = pl.multiple_of(i * rows, rows)
        cell = cells[pl.ds(base, rows), :]
        near = group_of[pl.ds(base, rows), :] - tile * TILE
        inside = (near >= 0) & (near < TILE)
        place = jnp.where(inside, near + (cell // HALF) * TILE, -1).astype(jnp.float32)
        inner = (cell % HALF).astype(jnp.float32)
        lefts, rights = [], []
        for j in range(rows):
            lanes = pl.ds(pl.multiple_of(i * BLOCK + j * 128, 128), 128)
            w = weights[:, lanes].astype(jnp.float32)
            here = jnp.broadcast_to(place[j : j + 1, :], (2 * TILE, 128)).astype(jnp.bfloat16)
            rights.append(jnp.where(here == slot, one, zero))
            mask = jnp.broadcast_to(inner[j : j + 1, :], (HALF, 128)).astype(jnp.bfloat16) == low_slot
            lefts.append(
                jnp.concatenate(
                    [
                        jnp.where(
                            mask,
                            jnp.broadcast_to(w[r : r + 1, :], (HALF, 128)).astype(jnp.bfloat16),
                            nothing,
                        )
                        for r in range(reps)
                    ],
                    axis=0,
                )
            )
        left = jnp.concatenate(lefts, axis=1)
        right = jnp.concatenate(rights, axis=1)
        total[...] += lax.dot_general(
            left, right, (((1,), (1,)), ((), ())), preferred_element_type=jnp.float32
        )
        return carry

    lax.fori_loop(low[tile], high[tile], add_block, 0)
    for r in range(reps):
        for h in range(2):
            out[r * CELLS + h * HALF : r * CELLS + (h + 1) * HALF, :] = total[
                r * HALF : (r + 1) * HALF, h * TILE : (h + 1) * TILE
            ]


def tabulate(weights, cell_ids, group_sizes):
    reps, records = weights.shape
    groups = group_sizes.shape[1]
    blocks = records // BLOCK
    group_range = jnp.arange(groups, dtype=jnp.int32)
    upper = (group_range[:, None] <= group_range[None, :]).astype(jnp.float32)
    ends = exact_dot(group_sizes.astype(jnp.float32), upper)[0].astype(jnp.int32)
    starts = ends - group_sizes[0]
    edge = jnp.arange(blocks, dtype=jnp.int32) * BLOCK
    first = jnp.sum((ends[None, :] <= edge[:, None]).astype(jnp.int32), axis=1)
    low = starts[::TILE] // BLOCK
    high = (ends[TILE - 1 :: TILE] + BLOCK - 1) // BLOCK
    starts = jnp.concatenate([starts, jnp.full((128,), records + 1, jnp.int32)])
    smem = pl.BlockSpec(memory_space=pltpu.SMEM)
    return pl.pallas_call(
        tabulate_kernel,
        out_shape=jax.ShapeDtypeStruct((reps * CELLS, groups), jnp.float32),
        grid=(groups // TILE,),
        in_specs=[
            smem,
            smem,
            smem,
            smem,
            pl.BlockSpec((reps, records), lambda t: (0, 0)),
            pl.BlockSpec((records // 128, 128), lambda t: (0, 0)),
        ],
        out_specs=pl.BlockSpec((reps * CELLS, TILE), lambda t: (0, t)),
        scratch_shapes=[
            pltpu.VMEM((records // 128, 128), jnp.int32),
            pltpu.VMEM((reps * HALF, 2 * TILE), jnp.float32),
        ],
        compiler_params=pltpu.CompilerParams(vmem_limit_bytes=40 * 1024 * 1024),
    )(starts, first, low, high, weights, cell_ids.reshape(records // 128, 128))


def pieces(value):
    upper = value.astype(jnp.bfloat16)
    lower = (value - upper.astype(jnp.float32)).astype(jnp.bfloat16)
    return upper, lower


def rake(columns, goals, reps):
    cells = columns[: reps * CELLS, :].reshape(reps, AGES, KINDS, 128)
    member = columns[reps * CELLS : reps * CELLS + 8, :]
    ages = [(goals[a : a + 1, :] * member[0:1, :]).reshape(1, 1, 128) for a in range(AGES)]
    kinds = (goals[8:16, :] * member).reshape(1, KINDS, 128)
    current = [cells[:, a] for a in range(AGES)]
    by_age = [jnp.ones((reps, 1, 128), jnp.float32) for _ in range(AGES)]
    by_kind = jnp.ones((reps, KINDS, 128), jnp.float32)
    for _ in range(ITERS):
        for a in range(AGES):
            ratio = ages[a] / jnp.maximum(jnp.sum(current[a], axis=1, keepdims=True), 1.0)
            current[a] = current[a] * ratio
            by_age[a] = by_age[a] * ratio
        ratio = kinds / jnp.maximum(current[0] + current[1] + current[2] + current[3], 1.0)
        current = [c * ratio for c in current]
        by_kind = by_kind * ratio
    row = lax.broadcasted_iota(jnp.int32, (reps, 8, 128), 1)
    ages_full = jnp.broadcast_to(by_age[3], (reps, 8, 128))
    for a in range(AGES - 1):
        ages_full = jnp.where(row == a, by_age[a], ages_full)
    return jnp.concatenate([ages_full, by_kind], axis=1).reshape(reps * 16, 128)


def finish_kernel(
    owners, parts, tables, county, goals, raked, spread,
    hot, partial, inbox, factors, picked, moments, arrived, shares,
    sum_send, sum_recv, factor_send, factor_recv, part_send, part_recv, share_send, share_recv,
):
    me = lax.axis_index("rows")
    mine = lax.axis_index("rep")
    width, groups = tables.shape
    reps = width // CELLS
    counties = hot.shape[0]
    here = counties // owners
    quarter = groups // parts
    barrier = pltpu.get_barrier_semaphore()
    for d in range(1, owners):
        pl.semaphore_signal(barrier, inc=1, device_id={"rows": lax.rem(me + d, owners)}, device_id_type=MESH)
    for d in range(1, parts):
        pl.semaphore_signal(barrier, inc=1, device_id={"rep": lax.rem(mine + d, parts)}, device_id_type=MESH)

    ids = lax.broadcasted_iota(jnp.int32, (counties, groups), 0)
    is_member = (ids == jnp.broadcast_to(county[...], (counties, groups))).astype(jnp.float32)
    hot[...] = is_member.astype(jnp.bfloat16)
    partial[:, width:] = jnp.broadcast_to(jnp.sum(is_member, axis=1, keepdims=True), (counties, 128))
    upper, lower = pieces(tables[...])
    contract = (((1,), (1,)), ((), ()))
    partial[:, :width] = lax.dot_general(
        hot[...], upper, contract, preferred_element_type=jnp.float32
    ) + lax.dot_general(hot[...], lower, contract, preferred_element_type=jnp.float32)
    pl.semaphore_wait(barrier, owners - 1 + parts - 1)

    def rows_of(owner):
        return pl.ds(pl.multiple_of(owner * here, here), here)

    def lanes_of(part):
        return pl.ds(pl.multiple_of(part * quarter, quarter), quarter)

    sums = []
    for d in range(1, owners):
        target = lax.rem(me + d, owners)
        copy = pltpu.make_async_remote_copy(
            src_ref=partial.at[rows_of(target)],
            dst_ref=inbox.at[d - 1],
            send_sem=sum_send.at[d - 1],
            recv_sem=sum_recv.at[d - 1],
            device_id={"rows": target},
            device_id_type=MESH,
        )
        copy.start()
        sums.append(copy)
    total = partial[rows_of(me), :]
    for d in range(1, owners):
        sums[d - 1].wait_recv()
        total = total + inbox[d - 1]
    columns = jnp.concatenate([total, jnp.zeros((128 - here, width + 128), jnp.float32)], axis=0).T
    found = rake(columns, goals[...], reps)
    room = factors.shape[1]
    found = jnp.concatenate([found, jnp.zeros((room - reps * 16, 128), jnp.float32)], axis=0)
    factors[rows_of(me), :] = found.T[:here, :]
    gathers = []
    for d in range(1, owners):
        target = lax.rem(me + d, owners)
        copy = pltpu.make_async_remote_copy(
            src_ref=factors.at[rows_of(me)],
            dst_ref=factors.at[rows_of(me)],
            send_sem=factor_send.at[d - 1],
            recv_sem=factor_recv.at[d - 1],
            device_id={"rows": target},
            device_id_type=MESH,
        )
        copy.start()
        gathers.append(copy)
    for copy in gathers:
        copy.wait_recv()
    upper, lower = pieces(factors[...].T)
    picked[...] = jnp.dot(upper, hot[...], preferred_element_type=jnp.float32) + jnp.dot(
        lower, hot[...], preferred_element_type=jnp.float32
    )

    def work(part):
        for t in range(quarter // 128):
            lanes = pl.ds(pl.multiple_of(part * quarter + t * 128, 128), 128)
            inner = pl.ds(t * 128, 128)
            count = [jnp.zeros((8, 128), jnp.float32) for _ in range(AGES)]
            for r in range(reps):
                by_age = picked[r * 16 : r * 16 + 8, lanes]
                by_kind = picked[r * 16 + 8 : r * 16 + 16, lanes]
                for a in range(AGES):
                    at = r * CELLS + a * 8
                    value = tables[at : at + 8, lanes] * (by_kind * by_age[a : a + 1, :])
                    raked[at : at + 8, lanes] = value
                    count[a] = count[a] + value
            for a in range(AGES):
                mean = count[a] / reps
                within = jnp.zeros((8, 128), jnp.float32)
                for r in range(reps):
                    at = r * CELLS + a * 8
                    within = within + jnp.square(raked[at : at + 8, lanes] - mean)
                moments[part, a * 8 : a * 8 + 8, inner] = mean
                moments[part, CELLS + a * 8 : CELLS + a * 8 + 8, inner] = within

    sends = []
    for d in range(1, parts):
        target = lax.rem(mine + d, parts)
        work(target)
        copy = pltpu.make_async_remote_copy(
            src_ref=moments.at[target],
            dst_ref=arrived.at[d - 1],
            send_sem=part_send.at[d - 1],
            recv_sem=part_recv.at[d - 1],
            device_id={"rep": target},
            device_id_type=MESH,
        )
        copy.start()
        sends.append(copy)
    work(mine)
    own = moments[mine]
    both = [own]
    for d in range(1, parts):
        sends[d - 1].wait_recv()
        both.append(arrived[d - 1])
    centre = both[0][:CELLS]
    for other in both[1:]:
        centre = centre + other[:CELLS]
    centre = centre / parts
    deviation = jnp.zeros((CELLS, quarter), jnp.float32)
    for other in both:
        deviation = deviation + (other[CELLS:] + reps * jnp.square(other[:CELLS] - centre))
    shares[mine] = deviation * (4.0 / (reps * parts))
    answers = []
    for d in range(1, parts):
        target = lax.rem(mine + d, parts)
        copy = pltpu.make_async_remote_copy(
            src_ref=shares.at[mine],
            dst_ref=shares.at[mine],
            send_sem=share_send.at[d - 1],
            recv_sem=share_recv.at[d - 1],
            device_id={"rep": target},
            device_id_type=MESH,
        )
        copy.start()
        answers.append(copy)
    for copy in answers:
        copy.wait_recv()
    for part in range(parts):
        spread[:, part * quarter : (part + 1) * quarter] = shares[part]
    for copy in sums + gathers + sends + answers:
        copy.wait_send()


def local(weights, cell_ids, group_sizes, group_county, age_rate, kind_rate):
    owners, parts = lax.axis_size("rows"), lax.axis_size("rep")
    tables = tabulate(weights, cell_ids, group_sizes)
    width, groups = tables.shape
    here = age_rate.shape[0]
    counties = here * owners
    room = -(-(width // 2) // 128) * 128
    goals = jnp.concatenate([age_rate.T, jnp.zeros((8 - AGES, here), jnp.float32), kind_rate.T], axis=0)
    goals = jnp.pad(goals, ((0, 0), (0, 128 - here)))
    quarter = groups // parts
    vmem = pl.BlockSpec(memory_space=pltpu.VMEM)
    dma = pltpu.SemaphoreType.DMA
    raked, spread = pl.pallas_call(
        functools.partial(finish_kernel, owners, parts),
        out_shape=(
            jax.ShapeDtypeStruct((width, groups), jnp.float32),
            jax.ShapeDtypeStruct((CELLS, groups), jnp.float32),
        ),
        in_specs=[vmem] * 3,
        out_specs=(vmem, vmem),
        scratch_shapes=[
            pltpu.VMEM((counties, groups), jnp.bfloat16),
            pltpu.VMEM((counties, width + 128), jnp.float32),
            pltpu.VMEM((owners - 1, here, width + 128), jnp.float32),
            pltpu.VMEM((counties, room), jnp.float32),
            pltpu.VMEM((room, groups), jnp.float32),
            pltpu.VMEM((parts, 2 * CELLS, quarter), jnp.float32),
            pltpu.VMEM((parts - 1, 2 * CELLS, quarter), jnp.float32),
            pltpu.VMEM((parts, CELLS, quarter), jnp.float32),
            dma((owners - 1,)),
            dma((owners - 1,)),
            dma((owners - 1,)),
            dma((owners - 1,)),
            dma((parts - 1,)),
            dma((parts - 1,)),
            dma((parts - 1,)),
            dma((parts - 1,)),
        ],
        compiler_params=pltpu.CompilerParams(
            collective_id=0, has_side_effects=True, vmem_limit_bytes=48 * 1024 * 1024
        ),
    )(tables, group_county.reshape(1, groups), goals)
    return raked.T, spread.T


def solution(mesh):
    placed = (
        P("rep", "rows"),
        P("rows"),
        P("rows", None),
        P("rows", None),
        P("rows", None),
        P("rows", None),
    )
    return jax.shard_map(
        local,
        mesh=mesh,
        in_specs=placed,
        out_specs=(P("rows", "rep"), P("rows", None)),
        check_vma=False,
    )
```

```python
import functools

import jax
import jax.numpy as jnp
from jax import lax
from jax.experimental import pallas as pl
from jax.experimental.pallas import tpu as pltpu
from jax.sharding import PartitionSpec as P

AGES = 4
KINDS = 8
CELLS = 32
LOW = 32
ITERS = 4
UNIT = 1024
STEP = 3
CUT = 12
HALF = CELLS // 2
TILE = 128
MESH = pl.DeviceIdType.MESH


def exact_dot(left, right):
    return jnp.dot(left, right, precision=lax.Precision.HIGHEST, preferred_element_type=jnp.float32)


def tabulate_kernel(starts, first, weights, cells, out, columns, inners):
    reps, records = weights.shape
    groups = out.shape[1]
    out[...] = jnp.zeros_like(out)
    slot = lax.broadcasted_iota(jnp.int32, (2 * TILE, 128), 0).astype(jnp.float32).astype(jnp.bfloat16)
    low_slot = lax.broadcasted_iota(jnp.int32, (HALF, 128), 0).astype(jnp.float32).astype(jnp.bfloat16)
    one = jnp.ones((2 * TILE, 128), jnp.bfloat16)
    zero = jnp.zeros((2 * TILE, 128), jnp.bfloat16)
    nothing = jnp.zeros((HALF, 128), jnp.bfloat16)
    place0 = lax.broadcasted_iota(jnp.int32, (8, 128), 0) * 128 + lax.broadcasted_iota(jnp.int32, (8, 128), 1)
    lane = lax.broadcasted_iota(jnp.int32, (reps * HALF, TILE), 1)

    def name(at, carry):
        place = place0 + at * UNIT
        g0 = first[at]
        counts = [jnp.full((8, 128), g0, jnp.int32)] + [jnp.zeros((8, 128), jnp.int32)] * 3
        for j in range(UNIT // LOW):
            counts[j % 4] = counts[j % 4] + (place >= starts[g0 + 1 + j]).astype(jnp.int32)
        count = (counts[0] + counts[1]) + (counts[2] + counts[3])
        rows = pl.ds(pl.multiple_of(at * 8, 8), 8)
        cell = cells[rows, :]
        columns[rows, :] = (count % TILE + (cell // HALF) * TILE).astype(jnp.float32)
        inners[rows, :] = (cell % HALF).astype(jnp.float32)
        return carry

    lax.fori_loop(0, records // UNIT, name, 0, unroll=2)

    def add_block(unit, units):
        lefts, rights = [], []
        for u in range(units):
            at = unit + u
            column = columns[pl.ds(pl.multiple_of(at * 8, 8), 8), :]
            inner = inners[pl.ds(pl.multiple_of(at * 8, 8), 8), :]
            for j in range(8):
                lanes = pl.ds(pl.multiple_of(at * UNIT + j * 128, 128), 128)
                w = weights[:, lanes].astype(jnp.float32)
                here = jnp.broadcast_to(column[j : j + 1, :], (2 * TILE, 128)).astype(jnp.bfloat16)
                rights.append(jnp.where(here == slot, one, zero))
                mask = jnp.broadcast_to(inner[j : j + 1, :], (HALF, 128)).astype(jnp.bfloat16) == low_slot
                lefts.append(
                    jnp.concatenate(
                        [
                            jnp.where(
                                mask,
                                jnp.broadcast_to(w[r : r + 1, :], (HALF, 128)).astype(jnp.bfloat16),
                                nothing,
                            )
                            for r in range(reps)
                        ],
                        axis=0,
                    )
                )
        found = lax.dot_general(
            jnp.concatenate(lefts, axis=1),
            jnp.concatenate(rights, axis=1),
            (((1,), (1,)), ((), ())),
            preferred_element_type=jnp.float32,
        )
        g0 = first[unit]
        tile = g0 // TILE
        following = jnp.minimum(tile + 1, groups // TILE - 1)
        wrapped = lane < g0 % TILE
        for h in range(2):
            half = found[:, h * TILE : (h + 1) * TILE]
            for where, part in (
                (tile, jnp.where(wrapped, 0.0, half)),
                (following, jnp.where(wrapped, half, 0.0)),
            ):
                lanes = pl.ds(pl.multiple_of(where * TILE, TILE), TILE)
                for r in range(reps):
                    at = r * CELLS + h * HALF
                    out[at : at + HALF, lanes] += part[r * HALF : (r + 1) * HALF, :]

    units = records // UNIT
    whole = units // STEP

    def step(i, carry):
        add_block(i * STEP, STEP)
        return carry

    lax.fori_loop(0, whole, step, 0)
    if units % STEP:
        add_block(whole * STEP, units % STEP)


def tabulate(weights, cell_ids, group_sizes):
    reps, records = weights.shape
    groups = group_sizes.shape[1]
    group_range = jnp.arange(groups, dtype=jnp.int32)
    upper = (group_range[:, None] <= group_range[None, :]).astype(jnp.float32)
    ends = exact_dot(group_sizes.astype(jnp.float32), upper)[0].astype(jnp.int32)
    starts = ends - group_sizes[0]
    edge = jnp.arange(records // UNIT, dtype=jnp.int32) * UNIT
    first = jnp.sum((ends[None, :] <= edge[:, None]).astype(jnp.int32), axis=1)
    starts = jnp.concatenate([starts, jnp.full((128,), records + 1, jnp.int32)])
    smem = pl.BlockSpec(memory_space=pltpu.SMEM)
    vmem = pl.BlockSpec(memory_space=pltpu.VMEM)
    return pl.pallas_call(
        tabulate_kernel,
        out_shape=jax.ShapeDtypeStruct((reps * CELLS, groups), jnp.float32),
        in_specs=[smem, smem, vmem, vmem],
        out_specs=vmem,
        scratch_shapes=[pltpu.VMEM((records // 128, 128), jnp.float32)] * 2,
        compiler_params=pltpu.CompilerParams(vmem_limit_bytes=40 * 1024 * 1024),
    )(starts, first, weights, cell_ids.reshape(records // 128, 128))


def pieces(value):
    upper = value.astype(jnp.bfloat16)
    lower = (value - upper.astype(jnp.float32)).astype(jnp.bfloat16)
    return upper, lower


def rake(columns, member, goals):
    reps = columns.shape[0] // CELLS
    cells = columns.reshape(reps, AGES, KINDS, 128)
    ages = [(goals[a : a + 1, :] * member[0:1, :]).reshape(1, 1, 128) for a in range(AGES)]
    kinds = (goals[8:16, :] * member).reshape(1, KINDS, 128)
    current = [cells[:, a] for a in range(AGES)]
    by_age = [jnp.ones((reps, 1, 128), jnp.float32) for _ in range(AGES)]
    by_kind = jnp.ones((reps, KINDS, 128), jnp.float32)
    for _ in range(ITERS):
        for a in range(AGES):
            ratio = ages[a] / jnp.maximum(jnp.sum(current[a], axis=1, keepdims=True), 1.0)
            current[a] = current[a] * ratio
            by_age[a] = by_age[a] * ratio
        ratio = kinds / jnp.maximum(current[0] + current[1] + current[2] + current[3], 1.0)
        current = [c * ratio for c in current]
        by_kind = by_kind * ratio
    row = lax.broadcasted_iota(jnp.int32, (reps, 8, 128), 1)
    ages_full = jnp.broadcast_to(by_age[3], (reps, 8, 128))
    for a in range(AGES - 1):
        ages_full = jnp.where(row == a, by_age[a], ages_full)
    return jnp.concatenate([ages_full, by_kind], axis=1).reshape(reps * 16, 128)


def finish_kernel(
    owners, parts, tables, county, goals, raked, spread,
    hot, partial_a, partial_b, inbox_a, inbox_b, factors_a, factors_b, picked, moments, arrived, shares,
    sum_send, sum_recv, factor_send, factor_recv, part_send, part_recv, share_send, share_recv,
):
    me = lax.axis_index("rows")
    mine = lax.axis_index("rep")
    width, groups = tables.shape
    reps = width // CELLS
    counties = hot.shape[0]
    here = counties // owners
    quarter = groups // parts
    barrier = pltpu.get_barrier_semaphore()
    for d in range(1, owners):
        pl.semaphore_signal(barrier, inc=1, device_id={"rows": lax.rem(me + d, owners)}, device_id_type=MESH)
    for d in range(1, parts):
        pl.semaphore_signal(barrier, inc=1, device_id={"rep": lax.rem(mine + d, parts)}, device_id_type=MESH)

    ids = lax.broadcasted_iota(jnp.int32, (counties, groups), 0)
    is_member = (ids == jnp.broadcast_to(county[...], (counties, groups))).astype(jnp.float32)
    hot[...] = is_member.astype(jnp.bfloat16)
    partial_a[:, CUT * CELLS :] = jnp.broadcast_to(jnp.sum(is_member, axis=1, keepdims=True), (counties, 128))
    contract = (((1,), (1,)), ((), ()))

    def county_sums(low, high):
        upper, lower = pieces(tables[low * CELLS : high * CELLS, :])
        return lax.dot_general(
            hot[...], upper, contract, preferred_element_type=jnp.float32
        ) + lax.dot_general(hot[...], lower, contract, preferred_element_type=jnp.float32)

    def rows_of(owner):
        return pl.ds(pl.multiple_of(owner * here, here), here)

    def send_sums(partial, inbox, half):
        copies = []
        for d in range(1, owners):
            target = lax.rem(me + d, owners)
            copy = pltpu.make_async_remote_copy(
                src_ref=partial.at[rows_of(target)],
                dst_ref=inbox.at[d - 1],
                send_sem=sum_send.at[half, d - 1],
                recv_sem=sum_recv.at[half, d - 1],
                device_id={"rows": target},
                device_id_type=MESH,
            )
            copy.start()
            copies.append(copy)
        return copies

    def receive_sums(partial, inbox, copies):
        total = partial[rows_of(me), :]
        for d in range(1, owners):
            copies[d - 1].wait_recv()
            total = total + inbox[d - 1]
        return jnp.concatenate([total, jnp.zeros((128 - here, total.shape[1]), jnp.float32)], axis=0).T

    def send_factors(found, factors, half):
        room = factors.shape[1]
        if room > found.shape[0]:
            found = jnp.concatenate([found, jnp.zeros((room - found.shape[0], 128), jnp.float32)], axis=0)
        factors[rows_of(me), :] = found.T[:here, :]
        copies = []
        for d in range(1, owners):
            copy = pltpu.make_async_remote_copy(
                src_ref=factors.at[rows_of(me)],
                dst_ref=factors.at[rows_of(me)],
                send_sem=factor_send.at[half, d - 1],
                recv_sem=factor_recv.at[half, d - 1],
                device_id={"rows": lax.rem(me + d, owners)},
                device_id_type=MESH,
            )
            copy.start()
            copies.append(copy)
        return copies

    def pick(factors, copies, low, high):
        for copy in copies:
            copy.wait_recv()
        upper, lower = pieces(factors[...].T)
        found = jnp.dot(upper, hot[...], preferred_element_type=jnp.float32) + jnp.dot(
            lower, hot[...], preferred_element_type=jnp.float32
        )
        picked[low * 16 : high * 16, :] = found[: (high - low) * 16, :]

    partial_a[:, : CUT * CELLS] = county_sums(0, CUT)
    pl.semaphore_wait(barrier, owners - 1 + parts - 1)
    sums_a = send_sums(partial_a, inbox_a, 0)
    partial_b[...] = county_sums(CUT, reps)
    sums_b = send_sums(partial_b, inbox_b, 1)
    columns = receive_sums(partial_a, inbox_a, sums_a)
    member = columns[CUT * CELLS : CUT * CELLS + 8, :]
    gathers_a = send_factors(rake(columns[: CUT * CELLS, :], member, goals[...]), factors_a, 0)
    columns = receive_sums(partial_b, inbox_b, sums_b)
    gathers_b = send_factors(rake(columns, member, goals[...]), factors_b, 1)
    pick(factors_a, gathers_a, 0, CUT)
    pick(factors_b, gathers_b, CUT, reps)
    sums, gathers = sums_a + sums_b, gathers_a + gathers_b

    def work(part):
        for t in range(quarter // 128):
            lanes = pl.ds(pl.multiple_of(part * quarter + t * 128, 128), 128)
            inner = pl.ds(t * 128, 128)
            count = [jnp.zeros((8, 128), jnp.float32) for _ in range(AGES)]
            for r in range(reps):
                by_age = picked[r * 16 : r * 16 + 8, lanes]
                by_kind = picked[r * 16 + 8 : r * 16 + 16, lanes]
                for a in range(AGES):
                    at = r * CELLS + a * 8
                    value = tables[at : at + 8, lanes] * (by_kind * by_age[a : a + 1, :])
                    raked[at : at + 8, lanes] = value
                    count[a] = count[a] + value
            for a in range(AGES):
                mean = count[a] / reps
                within = jnp.zeros((8, 128), jnp.float32)
                for r in range(reps):
                    at = r * CELLS + a * 8
                    within = within + jnp.square(raked[at : at + 8, lanes] - mean)
                moments[part, a * 8 : a * 8 + 8, inner] = mean
                moments[part, CELLS + a * 8 : CELLS + a * 8 + 8, inner] = within

    sends = []
    for d in range(1, parts):
        target = lax.rem(mine + d, parts)
        work(target)
        copy = pltpu.make_async_remote_copy(
            src_ref=moments.at[target],
            dst_ref=arrived.at[d - 1],
            send_sem=part_send.at[d - 1],
            recv_sem=part_recv.at[d - 1],
            device_id={"rep": target},
            device_id_type=MESH,
        )
        copy.start()
        sends.append(copy)
    work(mine)
    own = moments[mine]
    both = [own]
    for d in range(1, parts):
        sends[d - 1].wait_recv()
        both.append(arrived[d - 1])
    centre = both[0][:CELLS]
    for other in both[1:]:
        centre = centre + other[:CELLS]
    centre = centre / parts
    deviation = jnp.zeros((CELLS, quarter), jnp.float32)
    for other in both:
        deviation = deviation + (other[CELLS:] + reps * jnp.square(other[:CELLS] - centre))
    shares[mine] = deviation * (4.0 / (reps * parts))
    answers = []
    for d in range(1, parts):
        target = lax.rem(mine + d, parts)
        copy = pltpu.make_async_remote_copy(
            src_ref=shares.at[mine],
            dst_ref=shares.at[mine],
            send_sem=share_send.at[d - 1],
            recv_sem=share_recv.at[d - 1],
            device_id={"rep": target},
            device_id_type=MESH,
        )
        copy.start()
        answers.append(copy)
    for copy in answers:
        copy.wait_recv()
    for part in range(parts):
        spread[:, part * quarter : (part + 1) * quarter] = shares[part]
    for copy in sums + gathers + sends + answers:
        copy.wait_send()


def local(weights, cell_ids, group_sizes, group_county, age_rate, kind_rate):
    owners, parts = lax.axis_size("rows"), lax.axis_size("rep")
    tables = tabulate(weights, cell_ids, group_sizes)
    width, groups = tables.shape
    here = age_rate.shape[0]
    counties = here * owners
    cut_width = CUT * CELLS
    rest_width = width - cut_width
    goals = jnp.concatenate([age_rate.T, jnp.zeros((8 - AGES, here), jnp.float32), kind_rate.T], axis=0)
    goals = jnp.pad(goals, ((0, 0), (0, 128 - here)))
    quarter = groups // parts
    vmem = pl.BlockSpec(memory_space=pltpu.VMEM)
    dma = pltpu.SemaphoreType.DMA
    raked, spread = pl.pallas_call(
        functools.partial(finish_kernel, owners, parts),
        out_shape=(
            jax.ShapeDtypeStruct((width, groups), jnp.float32),
            jax.ShapeDtypeStruct((CELLS, groups), jnp.float32),
        ),
        in_specs=[vmem] * 3,
        out_specs=(vmem, vmem),
        scratch_shapes=[
            pltpu.VMEM((counties, groups), jnp.bfloat16),
            pltpu.VMEM((counties, cut_width + 128), jnp.float32),
            pltpu.VMEM((counties, rest_width), jnp.float32),
            pltpu.VMEM((owners - 1, here, cut_width + 128), jnp.float32),
            pltpu.VMEM((owners - 1, here, rest_width), jnp.float32),
            pltpu.VMEM((counties, -(-cut_width // 256) * 128), jnp.float32),
            pltpu.VMEM((counties, -(-rest_width // 256) * 128), jnp.float32),
            pltpu.VMEM((width // 2, groups), jnp.float32),
            pltpu.VMEM((parts, 2 * CELLS, quarter), jnp.float32),
            pltpu.VMEM((parts - 1, 2 * CELLS, quarter), jnp.float32),
            pltpu.VMEM((parts, CELLS, quarter), jnp.float32),
            dma((2, owners - 1)),
            dma((2, owners - 1)),
            dma((2, owners - 1)),
            dma((2, owners - 1)),
            dma((parts - 1,)),
            dma((parts - 1,)),
            dma((parts - 1,)),
            dma((parts - 1,)),
        ],
        compiler_params=pltpu.CompilerParams(
            collective_id=0, has_side_effects=True, vmem_limit_bytes=48 * 1024 * 1024
        ),
    )(tables, group_county.reshape(1, groups), goals)
    return raked.T, spread.T


def solution(mesh):
    placed = (
        P("rep", "rows"),
        P("rows"),
        P("rows", None),
        P("rows", None),
        P("rows", None),
        P("rows", None),
    )
    return jax.shard_map(
        local,
        mesh=mesh,
        in_specs=placed,
        out_specs=(P("rows", "rep"), P("rows", None)),
        check_vma=False,
    )
```

```python
import functools

import jax
import jax.numpy as jnp
from jax import lax
from jax.experimental import pallas as pl
from jax.experimental.pallas import tpu as pltpu
from jax.sharding import PartitionSpec as P

AGES = 4
KINDS = 8
CELLS = 32
LOW = 32
ITERS = 4
UNIT = 1024
STEP = 3
CUT = 12
HALF = CELLS // 2
TILE = 128
MESH = pl.DeviceIdType.MESH


def exact_dot(left, right):
    return jnp.dot(left, right, precision=lax.Precision.HIGHEST, preferred_element_type=jnp.float32)


def tabulate_kernel(starts, first, weights, cells, out, columns, inners):
    reps, records = weights.shape
    groups = out.shape[1]
    out[...] = jnp.zeros_like(out)
    slot = lax.broadcasted_iota(jnp.int32, (2 * TILE, 128), 0).astype(jnp.float32).astype(jnp.bfloat16)
    low_slot = lax.broadcasted_iota(jnp.int32, (HALF, 128), 0).astype(jnp.float32).astype(jnp.bfloat16)
    one = jnp.ones((2 * TILE, 128), jnp.bfloat16)
    zero = jnp.zeros((2 * TILE, 128), jnp.bfloat16)
    nothing = jnp.zeros((HALF, 128), jnp.bfloat16)
    place0 = lax.broadcasted_iota(jnp.int32, (8, 128), 0) * 128 + lax.broadcasted_iota(jnp.int32, (8, 128), 1)
    lane = lax.broadcasted_iota(jnp.int32, (reps * HALF, TILE), 1)

    def name(at, carry):
        place = place0 + at * UNIT
        g0 = first[at]
        counts = [jnp.full((8, 128), g0, jnp.int32)] + [jnp.zeros((8, 128), jnp.int32)] * 3
        for j in range(UNIT // LOW):
            counts[j % 4] = counts[j % 4] + (place >= starts[g0 + 1 + j]).astype(jnp.int32)
        count = (counts[0] + counts[1]) + (counts[2] + counts[3])
        rows = pl.ds(pl.multiple_of(at * 8, 8), 8)
        cell = cells[rows, :]
        columns[rows, :] = (count % TILE + (cell // HALF) * TILE).astype(jnp.float32)
        inners[rows, :] = (cell % HALF).astype(jnp.float32)
        return carry

    lax.fori_loop(0, records // UNIT, name, 0, unroll=2)

    def add_block(unit, units):
        lefts, rights = [], []
        for u in range(units):
            at = unit + u
            column = columns[pl.ds(pl.multiple_of(at * 8, 8), 8), :]
            inner = inners[pl.ds(pl.multiple_of(at * 8, 8), 8), :]
            for j in range(8):
                lanes = pl.ds(pl.multiple_of(at * UNIT + j * 128, 128), 128)
                w = weights[:, lanes].astype(jnp.float32)
                here = jnp.broadcast_to(column[j : j + 1, :], (2 * TILE, 128)).astype(jnp.bfloat16)
                rights.append(jnp.where(here == slot, one, zero))
                mask = jnp.broadcast_to(inner[j : j + 1, :], (HALF, 128)).astype(jnp.bfloat16) == low_slot
                lefts.append(
                    jnp.concatenate(
                        [
                            jnp.where(
                                mask,
                                jnp.broadcast_to(w[r : r + 1, :], (HALF, 128)).astype(jnp.bfloat16),
                                nothing,
                            )
                            for r in range(reps)
                        ],
                        axis=0,
                    )
                )
        found = lax.dot_general(
            jnp.concatenate(lefts, axis=1),
            jnp.concatenate(rights, axis=1),
            (((1,), (1,)), ((), ())),
            preferred_element_type=jnp.float32,
        )
        g0 = first[unit]
        tile = g0 // TILE
        following = jnp.minimum(tile + 1, groups // TILE - 1)
        wrapped = lane < g0 % TILE
        for h in range(2):
            half = found[:, h * TILE : (h + 1) * TILE]
            for where, part in (
                (tile, jnp.where(wrapped, 0.0, half)),
                (following, jnp.where(wrapped, half, 0.0)),
            ):
                lanes = pl.ds(pl.multiple_of(where * TILE, TILE), TILE)
                for r in range(reps):
                    at = r * CELLS + h * HALF
                    out[at : at + HALF, lanes] += part[r * HALF : (r + 1) * HALF, :]

    units = records // UNIT
    whole = units // STEP

    def step(i, carry):
        add_block(i * STEP, STEP)
        return carry

    lax.fori_loop(0, whole, step, 0, unroll=3)
    if units % STEP:
        add_block(whole * STEP, units % STEP)


def tabulate(weights, cell_ids, group_sizes):
    reps, records = weights.shape
    groups = group_sizes.shape[1]
    group_range = jnp.arange(groups, dtype=jnp.int32)
    upper = (group_range[:, None] <= group_range[None, :]).astype(jnp.float32)
    ends = exact_dot(group_sizes.astype(jnp.float32), upper)[0].astype(jnp.int32)
    starts = ends - group_sizes[0]
    edge = jnp.arange(records // UNIT, dtype=jnp.int32) * UNIT
    first = jnp.sum((ends[None, :] <= edge[:, None]).astype(jnp.int32), axis=1)
    starts = jnp.concatenate([starts, jnp.full((128,), records + 1, jnp.int32)])
    smem = pl.BlockSpec(memory_space=pltpu.SMEM)
    vmem = pl.BlockSpec(memory_space=pltpu.VMEM)
    return pl.pallas_call(
        tabulate_kernel,
        out_shape=jax.ShapeDtypeStruct((reps * CELLS, groups), jnp.float32),
        in_specs=[smem, smem, vmem, vmem],
        out_specs=vmem,
        scratch_shapes=[pltpu.VMEM((records // 128, 128), jnp.float32)] * 2,
        compiler_params=pltpu.CompilerParams(vmem_limit_bytes=40 * 1024 * 1024),
    )(starts, first, weights, cell_ids.reshape(records // 128, 128))


def pieces(value):
    upper = value.astype(jnp.bfloat16)
    lower = (value - upper.astype(jnp.float32)).astype(jnp.bfloat16)
    return upper, lower


def rake(columns, member, goals):
    reps = columns.shape[0] // CELLS
    cells = columns.reshape(reps, AGES, KINDS, 128)
    ages = [(goals[a : a + 1, :] * member[0:1, :]).reshape(1, 1, 128) for a in range(AGES)]
    kinds = (goals[8:16, :] * member).reshape(1, KINDS, 128)
    current = [cells[:, a] for a in range(AGES)]
    by_age = [jnp.ones((reps, 1, 128), jnp.float32) for _ in range(AGES)]
    by_kind = jnp.ones((reps, KINDS, 128), jnp.float32)
    for _ in range(ITERS):
        for a in range(AGES):
            ratio = ages[a] / jnp.maximum(jnp.sum(current[a], axis=1, keepdims=True), 1.0)
            current[a] = current[a] * ratio
            by_age[a] = by_age[a] * ratio
        ratio = kinds / jnp.maximum(current[0] + current[1] + current[2] + current[3], 1.0)
        current = [c * ratio for c in current]
        by_kind = by_kind * ratio
    row = lax.broadcasted_iota(jnp.int32, (reps, 8, 128), 1)
    ages_full = jnp.broadcast_to(by_age[3], (reps, 8, 128))
    for a in range(AGES - 1):
        ages_full = jnp.where(row == a, by_age[a], ages_full)
    return jnp.concatenate([ages_full, by_kind], axis=1).reshape(reps * 16, 128)


def finish_kernel(
    owners, parts, tables, county, goals, raked, spread,
    hot, partial_a, partial_b, inbox_a, inbox_b, factors_a, factors_b, picked, moments, arrived, shares,
    sum_send, sum_recv, factor_send, factor_recv, part_send, part_recv, share_send, share_recv,
):
    me = lax.axis_index("rows")
    mine = lax.axis_index("rep")
    width, groups = tables.shape
    reps = width // CELLS
    counties = hot.shape[0]
    here = counties // owners
    quarter = groups // parts
    barrier = pltpu.get_barrier_semaphore()
    for d in range(1, owners):
        pl.semaphore_signal(barrier, inc=1, device_id={"rows": lax.rem(me + d, owners)}, device_id_type=MESH)
    for d in range(1, parts):
        pl.semaphore_signal(barrier, inc=1, device_id={"rep": lax.rem(mine + d, parts)}, device_id_type=MESH)

    ids = lax.broadcasted_iota(jnp.int32, (counties, groups), 0)
    is_member = (ids == jnp.broadcast_to(county[...], (counties, groups))).astype(jnp.float32)
    hot[...] = is_member.astype(jnp.bfloat16)
    partial_a[:, CUT * CELLS :] = jnp.broadcast_to(jnp.sum(is_member, axis=1, keepdims=True), (counties, 128))
    contract = (((1,), (1,)), ((), ()))

    def county_sums(low, high):
        upper, lower = pieces(tables[low * CELLS : high * CELLS, :])
        return lax.dot_general(
            hot[...], upper, contract, preferred_element_type=jnp.float32
        ) + lax.dot_general(hot[...], lower, contract, preferred_element_type=jnp.float32)

    def rows_of(owner):
        return pl.ds(pl.multiple_of(owner * here, here), here)

    def send_sums(partial, inbox, half):
        copies = []
        for d in range(1, owners):
            target = lax.rem(me + d, owners)
            copy = pltpu.make_async_remote_copy(
                src_ref=partial.at[rows_of(target)],
                dst_ref=inbox.at[d - 1],
                send_sem=sum_send.at[half, d - 1],
                recv_sem=sum_recv.at[half, d - 1],
                device_id={"rows": target},
                device_id_type=MESH,
            )
            copy.start()
            copies.append(copy)
        return copies

    def receive_sums(partial, inbox, copies):
        total = partial[rows_of(me), :]
        for d in range(1, owners):
            copies[d - 1].wait_recv()
            total = total + inbox[d - 1]
        return jnp.concatenate([total, jnp.zeros((128 - here, total.shape[1]), jnp.float32)], axis=0).T

    def send_factors(found, factors, half):
        room = factors.shape[1]
        if room > found.shape[0]:
            found = jnp.concatenate([found, jnp.zeros((room - found.shape[0], 128), jnp.float32)], axis=0)
        factors[rows_of(me), :] = found.T[:here, :]
        copies = []
        for d in range(1, owners):
            copy = pltpu.make_async_remote_copy(
                src_ref=factors.at[rows_of(me)],
                dst_ref=factors.at[rows_of(me)],
                send_sem=factor_send.at[half, d - 1],
                recv_sem=factor_recv.at[half, d - 1],
                device_id={"rows": lax.rem(me + d, owners)},
                device_id_type=MESH,
            )
            copy.start()
            copies.append(copy)
        return copies

    def pick(factors, copies, low, high):
        for copy in copies:
            copy.wait_recv()
        upper, lower = pieces(factors[...].T)
        found = jnp.dot(upper, hot[...], preferred_element_type=jnp.float32) + jnp.dot(
            lower, hot[...], preferred_element_type=jnp.float32
        )
        picked[low * 16 : high * 16, :] = found[: (high - low) * 16, :]

    partial_a[:, : CUT * CELLS] = county_sums(0, CUT)
    pl.semaphore_wait(barrier, owners - 1 + parts - 1)
    sums_a = send_sums(partial_a, inbox_a, 0)
    partial_b[...] = county_sums(CUT, reps)
    sums_b = send_sums(partial_b, inbox_b, 1)
    columns = receive_sums(partial_a, inbox_a, sums_a)
    member = columns[CUT * CELLS : CUT * CELLS + 8, :]
    gathers_a = send_factors(rake(columns[: CUT * CELLS, :], member, goals[...]), factors_a, 0)
    columns = receive_sums(partial_b, inbox_b, sums_b)
    gathers_b = send_factors(rake(columns, member, goals[...]), factors_b, 1)
    pick(factors_a, gathers_a, 0, CUT)
    pick(factors_b, gathers_b, CUT, reps)
    sums, gathers = sums_a + sums_b, gathers_a + gathers_b

    def work(part):
        for t in range(quarter // 128):
            lanes = pl.ds(pl.multiple_of(part * quarter + t * 128, 128), 128)
            inner = pl.ds(t * 128, 128)
            count = [jnp.zeros((8, 128), jnp.float32) for _ in range(AGES)]
            for r in range(reps):
                by_age = picked[r * 16 : r * 16 + 8, lanes]
                by_kind = picked[r * 16 + 8 : r * 16 + 16, lanes]
                for a in range(AGES):
                    at = r * CELLS + a * 8
                    value = tables[at : at + 8, lanes] * (by_kind * by_age[a : a + 1, :])
                    raked[at : at + 8, lanes] = value
                    count[a] = count[a] + value
            for a in range(AGES):
                mean = count[a] / reps
                within = jnp.zeros((8, 128), jnp.float32)
                for r in range(reps):
                    at = r * CELLS + a * 8
                    within = within + jnp.square(raked[at : at + 8, lanes] - mean)
                moments[part, a * 8 : a * 8 + 8, inner] = mean
                moments[part, CELLS + a * 8 : CELLS + a * 8 + 8, inner] = within

    sends = []
    for d in range(1, parts):
        target = lax.rem(mine + d, parts)
        work(target)
        copy = pltpu.make_async_remote_copy(
            src_ref=moments.at[target],
            dst_ref=arrived.at[d - 1],
            send_sem=part_send.at[d - 1],
            recv_sem=part_recv.at[d - 1],
            device_id={"rep": target},
            device_id_type=MESH,
        )
        copy.start()
        sends.append(copy)
    work(mine)
    own = moments[mine]
    both = [own]
    for d in range(1, parts):
        sends[d - 1].wait_recv()
        both.append(arrived[d - 1])
    centre = both[0][:CELLS]
    for other in both[1:]:
        centre = centre + other[:CELLS]
    centre = centre / parts
    deviation = jnp.zeros((CELLS, quarter), jnp.float32)
    for other in both:
        deviation = deviation + (other[CELLS:] + reps * jnp.square(other[:CELLS] - centre))
    shares[mine] = deviation * (4.0 / (reps * parts))
    answers = []
    for d in range(1, parts):
        target = lax.rem(mine + d, parts)
        copy = pltpu.make_async_remote_copy(
            src_ref=shares.at[mine],
            dst_ref=shares.at[mine],
            send_sem=share_send.at[d - 1],
            recv_sem=share_recv.at[d - 1],
            device_id={"rep": target},
            device_id_type=MESH,
        )
        copy.start()
        answers.append(copy)
    for copy in answers:
        copy.wait_recv()
    for part in range(parts):
        spread[:, part * quarter : (part + 1) * quarter] = shares[part]
    for copy in sums + gathers + sends + answers:
        copy.wait_send()


def local(weights, cell_ids, group_sizes, group_county, age_rate, kind_rate):
    owners, parts = lax.axis_size("rows"), lax.axis_size("rep")
    tables = tabulate(weights, cell_ids, group_sizes)
    width, groups = tables.shape
    here = age_rate.shape[0]
    counties = here * owners
    cut_width = CUT * CELLS
    rest_width = width - cut_width
    goals = jnp.concatenate([age_rate.T, jnp.zeros((8 - AGES, here), jnp.float32), kind_rate.T], axis=0)
    goals = jnp.pad(goals, ((0, 0), (0, 128 - here)))
    quarter = groups // parts
    vmem = pl.BlockSpec(memory_space=pltpu.VMEM)
    dma = pltpu.SemaphoreType.DMA
    raked, spread = pl.pallas_call(
        functools.partial(finish_kernel, owners, parts),
        out_shape=(
            jax.ShapeDtypeStruct((width, groups), jnp.float32),
            jax.ShapeDtypeStruct((CELLS, groups), jnp.float32),
        ),
        in_specs=[vmem] * 3,
        out_specs=(vmem, vmem),
        scratch_shapes=[
            pltpu.VMEM((counties, groups), jnp.bfloat16),
            pltpu.VMEM((counties, cut_width + 128), jnp.float32),
            pltpu.VMEM((counties, rest_width), jnp.float32),
            pltpu.VMEM((owners - 1, here, cut_width + 128), jnp.float32),
            pltpu.VMEM((owners - 1, here, rest_width), jnp.float32),
            pltpu.VMEM((counties, -(-cut_width // 256) * 128), jnp.float32),
            pltpu.VMEM((counties, -(-rest_width // 256) * 128), jnp.float32),
            pltpu.VMEM((width // 2, groups), jnp.float32),
            pltpu.VMEM((parts, 2 * CELLS, quarter), jnp.float32),
            pltpu.VMEM((parts - 1, 2 * CELLS, quarter), jnp.float32),
            pltpu.VMEM((parts, CELLS, quarter), jnp.float32),
            dma((2, owners - 1)),
            dma((2, owners - 1)),
            dma((2, owners - 1)),
            dma((2, owners - 1)),
            dma((parts - 1,)),
            dma((parts - 1,)),
            dma((parts - 1,)),
            dma((parts - 1,)),
        ],
        compiler_params=pltpu.CompilerParams(
            collective_id=0, has_side_effects=True, vmem_limit_bytes=48 * 1024 * 1024
        ),
    )(tables, group_county.reshape(1, groups), goals)
    return raked.T, spread.T


def solution(mesh):
    placed = (
        P("rep", "rows"),
        P("rows"),
        P("rows", None),
        P("rows", None),
        P("rows", None),
        P("rows", None),
    )
    return jax.shard_map(
        local,
        mesh=mesh,
        in_specs=placed,
        out_specs=(P("rows", "rep"), P("rows", None)),
        check_vma=False,
    )
```
